32 devices in a mesh: dp: 8 (over y, x, core), tensor: 4 (over z).
Axes of the slice: x: 2, y: 2, z: 4, core: 2. Of those that a mesh axis runs over, the one named last changes fastest.
Arguments:
- hidden: bfloat16 [768, 2560], P('dp', 'tensor'), may hold values from -6 to 6
- grad_out: bfloat16 [768, 4096], P(('dp', 'tensor')), may hold values from -6 to 6
- base_down: bfloat16 [2560, 4096], P('tensor'), may hold values from -0.125 to 0.125
- adapter_in: bfloat16 [2560, 128], P('tensor'), may hold values from -0.125 to 0.125
- adapter_out: bfloat16 [128, 4096], replicated, may hold values from -0.09375 to 0.09375
- mix_ids: int32 [768], P('dp'), may hold values from 0 to 15
- comp_index: int32 [16, 2], replicated, may hold values from 0 to 7
- comp_coef: float32 [16, 2], replicated, may hold values from -1.5 to 1.5
Outputs:
- grad_hidden: bfloat16 [768, 2560], P('dp', 'tensor')
- grad_adapter_in: float32 [2560, 128], P('tensor')
- grad_adapter_out: float32 [128, 4096], replicated
The draws below stay inside these ranges and needn't reach their ends.
All inputs are finite; a program needn't handle non-finite values.
Results may differ from the reference program's by a relative error of at most 0.0034.
Values may be sent and summed in bfloat16 or wider, within the bound.
A program may use at most 64 MiB of HBM per device.

```python
import jax
import jax.numpy as jnp
from jax import lax

D = 4096
ADAPTERS = 8
RANK = 16
COMBOS = 16
PICKS = 2
R = 128
FF = 2560
TOKENS = 768


def set_ends(entries, key, low, largest):
    place = [jax.random.randint(jax.random.fold_in(key, axis), (), 0, length) for axis, length in enumerate(entries.shape)]
    widest = entries.shape.index(max(entries.shape))
    neighbour = place[:widest] + [(place[widest] + 1) % entries.shape[widest]] + place[widest + 1:]
    return entries.at[tuple(place)].set(low).at[tuple(neighbour)].set(largest)


def shard_levels(own_key, extent, split, smallest, largest):
    def one(position, blocks):
        steps = jax.random.uniform(jax.random.fold_in(jax.random.fold_in(own_key, 6), position), (blocks,), jnp.float32, smallest / len(split), largest / len(split))
        return jnp.repeat(jnp.exp(steps), extent[position] // blocks).reshape((-1,) + (1,) * (len(extent) - position - 1))

    loudness = one(*split[0])
    for cut in split[1:]:
        loudness = loudness * one(*cut)
    return loudness


def gaussian(rng, shape, width, reach, cuts=(), kind=jnp.bfloat16):
    array = width * jax.random.normal(rng, shape, jnp.float32)
    if cuts:
        array = array * shard_levels(rng, shape, cuts, -0.22, 0.18)
    return jnp.clip(array, -reach, reach).astype(kind)


def setup_inputs(seed: int = 0) -> dict:
    arg_keys = jax.random.split(jax.random.key(seed), 9)
    hidden = gaussian(arg_keys[0], (TOKENS, FF), 1.0, 6.0, ((0, 8), (1, 4)))
    grad_out = gaussian(arg_keys[1], (TOKENS, D), 1.0, 6.0, ((0, 32),))
    base_down = gaussian(arg_keys[2], (FF, D), FF ** -0.5, 0.125, ((0, 4),))
    adapter_in = gaussian(arg_keys[3], (FF, R), FF ** -0.5, 0.125, ((0, 4),))
    adapter_out = gaussian(arg_keys[4], (R, D), D ** -0.5, 0.09375)
    mix_ids = set_ends(jax.random.randint(arg_keys[5], (TOKENS,), 0, COMBOS), jax.random.fold_in(arg_keys[5], 1), 0, COMBOS - 1).astype(jnp.int32)
    comp_index = set_ends(jax.random.randint(arg_keys[6], (COMBOS, PICKS), 0, ADAPTERS), jax.random.fold_in(arg_keys[6], 1), 0, ADAPTERS - 1).astype(jnp.int32)
    comp_coef = jnp.clip(jax.random.uniform(arg_keys[7], (COMBOS, PICKS), jnp.float32, -1.5, 1.5), -1.5, 1.5)
    return dict(hidden=hidden, grad_out=grad_out, base_down=base_down, adapter_in=adapter_in, adapter_out=adapter_out, mix_ids=mix_ids, comp_index=comp_index, comp_coef=comp_coef)


def table_rows(mix_ids, comp_index, comp_coef):
    adapter_ids = jnp.arange(ADAPTERS, dtype=jnp.int32)
    coef_table = jnp.zeros((COMBOS, ADAPTERS), jnp.float32)
    for pick in range(PICKS):
        hits = (comp_index[:, pick:pick + 1] == adapter_ids[None, :]).astype(jnp.float32)
        coef_table = coef_table + comp_coef[:, pick:pick + 1] * hits
    one_hot = (mix_ids[:, None] == jnp.arange(COMBOS, dtype=jnp.int32)[None, :]).astype(jnp.float32)
    per_token = jnp.dot(one_hot, coef_table, precision=lax.Precision.HIGHEST)
    return jnp.repeat(per_token, RANK, axis=1)


def reference(hidden, grad_out, base_down, adapter_in, adapter_out, mix_ids, comp_index, comp_coef):
    grad_scale = float(TOKENS) ** -0.5
    mix = table_rows(mix_ids, comp_index, comp_coef)
    low_acts = jnp.dot(hidden, adapter_in, preferred_element_type=jnp.float32)
    acts = (low_acts * mix).astype(jnp.bfloat16)
    low_grads = (jnp.dot(grad_out, adapter_out.T, preferred_element_type=jnp.float32) * mix).astype(jnp.bfloat16)
    base_part = jnp.dot(grad_out, base_down.T, preferred_element_type=jnp.float32)
    side_part = jnp.dot(low_grads, adapter_in.T, preferred_element_type=jnp.float32)
    grad_hidden = (base_part + side_part).astype(jnp.bfloat16)
    grad_adapter_in = jnp.dot(hidden.T, low_grads, preferred_element_type=jnp.float32) * grad_scale
    grad_adapter_out = jnp.dot(acts.T, grad_out, preferred_element_type=jnp.float32) * grad_scale
    return grad_hidden, grad_adapter_in, grad_adapter_out
```

```python
import functools

import jax
import jax.numpy as jnp
from jax import lax
from jax.experimental import pallas as pl
from jax.experimental.pallas import tpu as pltpu
from jax.sharding import PartitionSpec as P

RANK = 16
COMBOS = 16
PICKS = 2
LANES = 128
ROWS = 16
F32 = jnp.float32
BF16 = jnp.bfloat16
MESH = pl.DeviceIdType.MESH


def each(count, body):
    if count <= 8:
        for i in range(count):
            body(i)
    else:
        pl.loop(0, count)(body)


def plan(nd, nt, width, r):
    piece_rows = min(nd, r // ROWS)
    piece_cols = nd // piece_rows
    chunks = max(c for c in range(1, nt + 1) if nt % c == 0 and width % (LANES * c * piece_cols) == 0)
    return piece_rows, piece_cols, chunks


def kernel(nd, nt, hid, go, bd, ain, aout, ids, cidx, ccoef,
           gh_out, a_out, b_out,
           hid_v, ain_v, aout_v, bd_v, gath, mix, lowp, lowr, lgg, actg, paf, pab, par, pbf, pbb, pbr, acc,
           loc, loc_go, loc_ao, loc_bd, low_s, low_r, gat_s, gat_r, lg_s, lg_r, act_s, act_r,
           ra_s, ra_r, rb_s, rb_r, aa_s, aa_r, bz_s, bz_r, bx_s, bx_r, bc_s, bc_r):
    d, z = lax.axis_index("dp"), lax.axis_index("tensor")
    tg, width = go.shape
    tokens, ff = hid.shape
    r = ain.shape[1]
    piece_rows, piece_cols, chunks = plan(nd, nt, width, r)
    dc = width // chunks
    dcp = dc // piece_cols
    zc = lax.rem(z, chunks)
    zbase = z - zc
    nc = nd // 2
    chip, core = d // 2, lax.rem(d, 2)
    a_rows = pab.shape[1]

    def columns(k):
        return pl.ds(pl.multiple_of(lax.rem(zc + k, chunks) * dc, LANES), dc)

    def zpeer(i):
        return lax.rem(z + i + 1, nt)

    def zfrom(i):
        return lax.rem(z + nt - i - 1, nt)

    def dpeer(i):
        return lax.rem(d + i + 1, nd)

    def dfrom(i):
        return lax.rem(d + nd - i - 1, nd)

    def remote(src, dst, send, recv, **where):
        return pltpu.make_async_remote_copy(
            src_ref=src, dst_ref=dst, send_sem=send, recv_sem=recv, device_id=where, device_id_type=MESH)

    c_hid = pltpu.make_async_copy(hid, hid_v, loc.at[0])
    c_ain = pltpu.make_async_copy(ain, ain_v, loc.at[1])

    def c_go(q):
        return pltpu.make_async_copy(go.at[:, columns(q)], gath.at[q, z], loc_go.at[q])

    def c_ao(q):
        return pltpu.make_async_copy(aout.at[:, columns(q)], aout_v.at[q], loc_ao.at[q])

    def c_bd(q):
        return pltpu.make_async_copy(bd.at[:, columns(q)], bd_v.at[q], loc_bd.at[q])

    c_hid.start()
    c_ain.start()
    each(chunks, lambda q: c_go(q).start())
    each(chunks, lambda q: c_ao(q).start())
    each(chunks, lambda q: c_bd(q).start())

    barrier = pltpu.get_barrier_semaphore()
    each(nt - 1, lambda i: pl.semaphore_signal(barrier, inc=1, device_id={"tensor": zpeer(i)}, device_id_type=MESH))
    each(nd - 1, lambda i: pl.semaphore_signal(barrier, inc=1, device_id={"dp": dpeer(i)}, device_id_type=MESH))

    row = lax.broadcasted_iota(jnp.int32, (r, COMBOS), 0)
    table = jnp.zeros((r, COMBOS), F32)
    for p in range(PICKS):
        first = cidx[p:p + 1, :] * RANK
        table = table + jnp.where((row >= first) & (row < first + RANK), ccoef[p:p + 1, :], 0.0)
    one_hot = (lax.broadcasted_iota(jnp.int32, (COMBOS, tokens), 0) == ids[...]).astype(F32)
    mix_t = jnp.dot(table, one_hot, precision=lax.Precision.HIGHEST, preferred_element_type=F32)
    mix[...] = mix_t.T.reshape(nt, tg, r)

    c_hid.wait()
    c_ain.wait()
    lowp[...] = jnp.dot(hid_v[...], ain_v[...], preferred_element_type=F32).reshape(nt, tg, r)
    each(chunks, lambda q: c_go(q).wait())

    pl.semaphore_wait(barrier, nt + nd - 2)

    def low_copy(i):
        return remote(lowp.at[zpeer(i)], lowr.at[i], low_s.at[i], low_r.at[i], tensor=zpeer(i))

    each(nt - 1, lambda i: low_copy(i).start())

    def gather_send(q, i):
        mine = lax.rem(lax.rem(zpeer(i), chunks) + q + chunks - zc, chunks)
        return remote(gath.at[mine, z], gath.at[q, z], gat_s.at[q, i], gat_r.at[q, i], tensor=zpeer(i))

    def gather_recv(q, i):
        return remote(gath.at[q, zfrom(i)], gath.at[q, zfrom(i)], gat_s.at[q, i], gat_r.at[q, i], tensor=zpeer(i))

    each(nt - 1, lambda i: gather_send(0, i).start())

    low = jnp.zeros((tg, r), F32)
    for q in range(chunks):
        c_ao(q).wait()
        low = low + lax.dot_general(gath[q, z], aout_v[q], (((1,), (1,)), ((), ())), preferred_element_type=F32)
    lgg[z] = low * mix[z]

    def lg_send(i):
        return remote(lgg.at[z], lgg.at[z], lg_s.at[i], lg_r.at[i], tensor=zpeer(i))

    def lg_recv(i):
        return remote(lgg.at[zfrom(i)], lgg.at[zfrom(i)], lg_s.at[i], lg_r.at[i], tensor=zpeer(i))

    each(nt - 1, lambda i: lg_send(i).start())

    actg[z] = lowp[z]

    def low_add(i):
        low_copy(i).wait_recv()
        actg[z] += lowr[i]

    each(nt - 1, low_add)
    actg[z] = actg[z] * mix[z]

    def act_send(i):
        return remote(actg.at[z], actg.at[z], act_s.at[i], act_r.at[i], tensor=zpeer(i))

    def act_recv(i):
        return remote(actg.at[zfrom(i)], actg.at[zfrom(i)], act_s.at[i], act_r.at[i], tensor=zpeer(i))

    each(nt - 1, lambda i: act_send(i).start())
    for q in range(1, chunks):
        each(nt - 1, lambda i: gather_send(q, i).start())

    each(nt - 1, lambda i: lg_recv(i).wait_recv())
    low_grads = lgg[...].reshape(tokens, r).astype(BF16)
    part_a = lax.dot_general(hid_v[...], low_grads, (((0,), (0,)), ((), ())), preferred_element_type=F32)
    if nd * a_rows != ff:
        part_a = jnp.concatenate([part_a, jnp.zeros((nd * a_rows - ff, r), F32)], axis=0)
    part_a = part_a.reshape(nd, a_rows, r)
    paf[...] = part_a
    pab[...] = part_a.astype(BF16)

    def ra_copy(i):
        return remote(pab.at[dpeer(i)], par.at[i], ra_s.at[i], ra_r.at[i], dp=dpeer(i))

    each(nd - 1, lambda i: ra_copy(i).start())

    each(nt - 1, lambda i: act_recv(i).wait_recv())
    each(nt - 1, lambda i: gather_recv(0, i).wait_recv())

    def gathered(q):
        return gath[q].astype(F32).reshape(tokens, dc).astype(BF16)

    acts = actg[...].reshape(tokens, r).astype(BF16)
    grads = gathered(0)
    part_b = lax.dot_general(acts, grads, (((0,), (0,)), ((), ())), preferred_element_type=F32)
    for i in range(nd):
        top, left = (i % piece_rows) * ROWS, (i // piece_rows) * dcp
        piece = part_b[top:top + ROWS, left:left + dcp]
        pbf[i] = piece
        pbb[i] = piece.astype(BF16)

    def rb_copy(i):
        return remote(pbb.at[dpeer(i)], pbr.at[i], rb_s.at[i], rb_r.at[i], dp=dpeer(i))

    each(nd - 1, lambda i: rb_copy(i).start())

    def product(q, grads):
        c_bd(q).wait()
        return lax.dot_general(grads, bd_v[q], (((1,), (1,)), ((), ())), preferred_element_type=F32)

    acc[...] = product(0, grads) + lax.dot_general(
        low_grads, ain_v[...], (((1,), (1,)), ((), ())), preferred_element_type=F32)

    def a_piece(owner):
        return a_out.at[pl.ds(pl.multiple_of(owner * a_rows, ROWS), a_rows), :]

    def aa_send(i):
        return remote(a_piece(d), a_piece(d), aa_s.at[i], aa_r.at[i], dp=dpeer(i))

    def aa_recv(i):
        return remote(a_piece(dfrom(i)), a_piece(dfrom(i)), aa_s.at[i], aa_r.at[i], dp=dpeer(i))

    def a_add(i):
        ra_copy(i).wait_recv()
        paf[d] += par[i].astype(F32)

    each(nd - 1, a_add)
    a_piece(d)[...] = paf[d].astype(BF16)
    each(nd - 1, lambda i: aa_send(i).start())

    def b_piece(owner_chip, owner_core, chunk):
        owner = owner_chip * 2 + owner_core
        top = pl.multiple_of(lax.rem(owner, piece_rows) * ROWS, ROWS)
        left = pl.multiple_of(chunk * dc + (owner // piece_rows) * dcp, LANES)
        return b_out.at[pl.ds(top, ROWS), pl.ds(left, dcp)]

    def chip_at(j):
        return lax.rem(chip + j, nc)

    def chunk_at(k):
        return lax.rem(zc + chunks - k, chunks)

    def b_add(i):
        rb_copy(i).wait_recv()
        pbf[d] += pbr[i].astype(F32)

    each(nd - 1, b_add)
    own_b = b_piece(chip, core, zc)
    own_b[...] = pbf[d].astype(BF16)

    def bz(k, part):
        return remote(part, part, bz_s.at[k], bz_r.at[k], tensor=zbase + lax.rem(zc + k + 1, chunks))

    def bx(j, k, part):
        return remote(part, part, bx_s.at[j, k], bx_r.at[j, k], dp=chip_at(j + 1) * 2 + core)

    def bc(j, k, part):
        return remote(part, part, bc_s.at[j, k], bc_r.at[j, k], dp=chip * 2 + 1 - core)

    each(chunks - 1, lambda k: bz(k, own_b).start())
    each(nc - 1, lambda j: bx(j, 0, own_b).start())
    bc(0, 0, own_b).start()

    if chunks > 1:
        each(nt - 1, lambda i: gather_recv(1, i).wait_recv())
        acc[...] += product(1, gathered(1))

    for k in range(1, chunks):
        part = b_piece(chip, core, chunk_at(k))
        bz(k - 1, part).wait_recv()
        each(nc - 1, lambda j: bx(j, k, part).start())
        bc(0, k, part).start()

    for q in range(2, chunks):
        each(nt - 1, lambda i: gather_recv(q, i).wait_recv())
        acc[...] += product(q, gathered(q))
    gh_out[...] = acc[...].astype(BF16)

    for k in range(chunks):
        def pass_on(j):
            part = b_piece(lax.rem(chip + nc - j - 1, nc), core, chunk_at(k))
            bx(j, k, part).wait_recv()
            bc(j + 1, k, part).start()

        each(nc - 1, pass_on)

    each(nd - 1, lambda i: aa_recv(i).wait_recv())
    for k in range(chunks):
        each(nc, lambda j: bc(j, k, b_piece(lax.rem(chip + nc - j, nc), 1 - core, chunk_at(k))).wait_recv())

    def z_sends(i):
        low_copy(i).wait_send()
        lg_send(i).wait_send()
        act_send(i).wait_send()
        for q in range(chunks):
            gather_send(q, i).wait_send()

    each(nt - 1, z_sends)

    def d_sends(i):
        ra_copy(i).wait_send()
        rb_copy(i).wait_send()
        aa_send(i).wait_send()

    each(nd - 1, d_sends)
    each(chunks - 1, lambda k: bz(k, own_b).wait_send())
    for k in range(chunks):
        each(nc - 1, lambda j: bx(j, k, b_piece(chip, core, chunk_at(k))).wait_send())
        each(nc, lambda j: bc(j, k, b_piece(lax.rem(chip + nc - j, nc), core, chunk_at(k))).wait_send())


def shards(nd, nt, hidden, grad_out, base_down, adapter_in, adapter_out, mix_ids, comp_index, comp_coef):
    tokens, ff = hidden.shape
    tg, width = grad_out.shape
    r = adapter_in.shape[1]
    piece_rows, piece_cols, chunks = plan(nd, nt, width, r)
    dc = width // chunks
    dcp = dc // piece_cols
    a_rows = -(-ff // (nd * ROWS)) * ROWS
    grad_scale = float(tokens * nd) ** (-0.5)
    hbm = pl.BlockSpec(memory_space=pl.ANY)
    vmem = pl.BlockSpec(memory_space=pltpu.VMEM)
    dma = pltpu.SemaphoreType.DMA
    zs, ds = max(nt - 1, 1), max(nd - 1, 1)
    scratch = [
        pltpu.VMEM((tokens, ff), BF16), pltpu.VMEM((ff, r), BF16), pltpu.VMEM((chunks, r, dc), BF16),
        pltpu.VMEM((chunks, ff, dc), BF16), pltpu.VMEM((chunks, nt, tg, dc), BF16),
        pltpu.VMEM((nt, tg, r), F32), pltpu.VMEM((nt, tg, r), F32), pltpu.VMEM((zs, tg, r), F32),
        pltpu.VMEM((nt, tg, r), F32), pltpu.VMEM((nt, tg, r), F32),
        pltpu.VMEM((nd, a_rows, r), F32), pltpu.VMEM((nd, a_rows, r), BF16), pltpu.VMEM((ds, a_rows, r), BF16),
        pltpu.VMEM((nd, ROWS, dcp), F32), pltpu.VMEM((nd, ROWS, dcp), BF16), pltpu.VMEM((ds, ROWS, dcp), BF16),
        pltpu.VMEM((tokens, ff), F32),
        dma((2,)), dma((chunks,)), dma((chunks,)), dma((chunks,)),
        dma((zs,)), dma((zs,)), dma((chunks, zs)), dma((chunks, zs)), dma((zs,)), dma((zs,)), dma((zs,)), dma((zs,)),
        dma((ds,)), dma((ds,)), dma((ds,)), dma((ds,)), dma((ds,)), dma((ds,)),
        dma((chunks,)), dma((chunks,)), dma((nd // 2, chunks)), dma((nd // 2, chunks)),
        dma((nd // 2, chunks)), dma((nd // 2, chunks)),
    ]
    grad_hidden, sum_a, sum_b = pl.pallas_call(
        functools.partial(kernel, nd, nt),
        out_shape=(
            jax.ShapeDtypeStruct((tokens, ff), BF16),
            jax.ShapeDtypeStruct((nd * a_rows, r), BF16),
            jax.ShapeDtypeStruct((r, width), BF16),
        ),
        in_specs=[hbm] * 5 + [vmem] * 3,
        out_specs=(vmem, vmem, vmem),
        scratch_shapes=scratch,
        compiler_params=pltpu.CompilerParams(
            collective_id=0, has_side_effects=True, vmem_limit_bytes=48 * 1024 * 1024),
    )(hidden, grad_out, base_down, adapter_in, adapter_out, mix_ids.reshape(1, tokens), comp_index.T, comp_coef.T)
    return grad_hidden, sum_a[:ff].astype(F32) * grad_scale, sum_b.astype(F32) * grad_scale


def solution(mesh):
    in_specs = (
        P("dp", "tensor"),
        P(("dp", "tensor"), None),
        P("tensor", None),
        P("tensor", None),
        P(),
        P("dp"),
        P(),
        P(),
    )
    out_specs = (P("dp", "tensor"), P("tensor", None), P())
    body = functools.partial(shards, mesh.shape["dp"], mesh.shape["tensor"])
    return jax.shard_map(body, mesh=mesh, in_specs=in_specs, out_specs=out_specs, check_vma=False)
```

```python
import functools

import jax
import jax.numpy as jnp
from jax import lax
from jax.experimental import pallas as pl
from jax.experimental.pallas import tpu as pltpu
from jax.sharding import PartitionSpec as P

RANK = 16
COMBOS = 16
PICKS = 2
LANES = 128
ROWS = 16
F32 = jnp.float32
BF16 = jnp.bfloat16
MESH = pl.DeviceIdType.MESH


def each(count, body):
    if count <= 8:
        for i in range(count):
            body(i)
    else:
        pl.loop(0, count)(body)


def plan(nd, nt, width, r):
    piece_rows = min(nd, r // ROWS)
    piece_cols = nd // piece_rows
    chunks = max(c for c in range(1, nt + 1) if nt % c == 0 and width % (LANES * c * piece_cols) == 0)
    return piece_rows, piece_cols, chunks


def kernel(nd, nt, hid, go, bd, ain, aout, ids, cidx, ccoef,
           gh_out, a_out, b_out,
           hid_v, ain_v, ids_v, cidx_v, ccoef_v, aout_v, bd_v, gath, mix, lowp, lowr, lgg, actg, paf, pab, par, pbf, pbb, pbr, acc,
           loc, loc_go, loc_ao, loc_bd, low_s, low_r, gat_s, gat_r, fwd_s, lg_s, lg_r, act_s, act_r,
           ra_s, ra_r, rb_s, rb_r, aa_s, aa_r, bz_s, bz_r, bx_s, bx_r, bc_s, bc_r):
    d, z = lax.axis_index("dp"), lax.axis_index("tensor")
    tg, width = go.shape
    tokens, ff = hid.shape
    r = ain.shape[1]
    piece_rows, piece_cols, chunks = plan(nd, nt, width, r)
    dc = width // chunks
    dcp = dc // piece_cols
    zc = lax.rem(z, chunks)
    zbase = z - zc
    nc = nd // 2
    chip, core = d // 2, lax.rem(d, 2)
    a_rows = pab.shape[1]

    half = (nt + 1) // 2
    turn = 1 - 2 * (z // half)

    def columns(k):
        return pl.ds(pl.multiple_of(lax.rem(zc + turn * k + chunks, chunks) * dc, LANES), dc)

    def zpeer(i):
        return lax.rem(z + i + 1, nt)

    def zfrom(i):
        return lax.rem(z + nt - i - 1, nt)

    def dpeer(i):
        return lax.rem(d + i + 1, nd)

    def dfrom(i):
        return lax.rem(d + nd - i - 1, nd)

    def remote(src, dst, send, recv, **where):
        return pltpu.make_async_remote_copy(
            src_ref=src, dst_ref=dst, send_sem=send, recv_sem=recv, device_id=where, device_id_type=MESH)

    c_hid = pltpu.make_async_copy(hid, hid_v, loc.at[0])
    c_ain = pltpu.make_async_copy(ain, ain_v, loc.at[1])

    def c_go(q):
        return pltpu.make_async_copy(go.at[:, columns(q)], gath.at[q, z], loc_go.at[q])

    def c_ao(q):
        return pltpu.make_async_copy(aout.at[:, columns(q)], aout_v.at[q], loc_ao.at[q])

    def c_bd(q):
        return pltpu.make_async_copy(bd.at[:, columns(q)], bd_v.at[q], loc_bd.at[q])

    small = [pltpu.make_async_copy(src, dst, loc.at[2 + n])
             for n, (src, dst) in enumerate(((ids, ids_v), (cidx, cidx_v), (ccoef, ccoef_v)))]
    c_hid.start()
    c_ain.start()
    for c in small:
        c.start()
    each(chunks, lambda q: c_go(q).start())
    each(chunks, lambda q: c_ao(q).start())
    each(chunks, lambda q: c_bd(q).start())

    barrier = pltpu.get_barrier_semaphore()
    each(nt - 1, lambda i: pl.semaphore_signal(barrier, inc=1, device_id={"tensor": zpeer(i)}, device_id_type=MESH))
    each(nd - 1, lambda i: pl.semaphore_signal(barrier, inc=1, device_id={"dp": dpeer(i)}, device_id_type=MESH))

    row = lax.broadcasted_iota(jnp.int32, (r, COMBOS), 0)
    table = jnp.zeros((r, COMBOS), F32)
    for c in small:
        c.wait()
    for p in range(PICKS):
        first = cidx_v[p:p + 1, :] * RANK
        table = table + jnp.where((row >= first) & (row < first + RANK), ccoef_v[p:p + 1, :], 0.0)
    one_hot = (lax.broadcasted_iota(jnp.int32, (COMBOS, tokens), 0) == ids_v[...]).astype(F32)
    mix_t = jnp.dot(table, one_hot, precision=lax.Precision.HIGHEST, preferred_element_type=F32)
    mix[...] = mix_t.T.reshape(nt, tg, r)

    c_hid.wait()
    c_ain.wait()
    lowp[...] = jnp.dot(hid_v[...], ain_v[...], preferred_element_type=F32).reshape(nt, tg, r)
    each(chunks, lambda q: c_go(q).wait())

    pl.semaphore_wait(barrier, nt + nd - 2)

    def low_copy(i):
        return remote(lowp.at[zpeer(i)], lowr.at[i], low_s.at[i], low_r.at[i], tensor=zpeer(i))

    each(nt - 1, lambda i: low_copy(i).start())

    def gather_send(q, i):
        there = zpeer(i)
        chunk = lax.rem(lax.rem(there, chunks) + (1 - 2 * (there // half)) * q + chunks, chunks)
        mine = lax.rem(turn * (chunk - zc) + chunks, chunks)
        return remote(gath.at[mine, z], gath.at[q, z], gat_s.at[q, i], gat_r.at[q, i], tensor=zpeer(i))

    def gather_recv(q, i):
        return remote(gath.at[q, zfrom(i)], gath.at[q, zfrom(i)], gat_s.at[q, i], gat_r.at[q, i], tensor=zpeer(i))

    def if_direct(q, i, act):
        if q == 0 or nt < 3:
            act()
        else:
            pl.when(jnp.logical_not(((z == 0) & (i == nt - 2)) | ((z == nt - 1) & (i == 0))))(act)

    def gather_start(q):
        each(nt - 1, lambda i: if_direct(q, i, lambda: gather_send(q, i).start()))

    def passing(q, act):
        if nt >= 3 and q + 1 < chunks:
            for side, (via, src, end, i) in enumerate(((nt - 2, 0, nt - 1, nt - 2), (1, nt - 1, 0, 0))):
                pl.when(z == via)(functools.partial(act, remote(
                    gath.at[q, src], gath.at[q + 1, src], fwd_s.at[q, side], gat_r.at[q + 1, i], tensor=end)))

    def arrive(q):
        each(nt - 1, lambda i: gather_recv(q, i).wait_recv())
        passing(q, lambda c: c.start())

    gather_start(0)

    low = jnp.zeros((tg, r), F32)
    for q in range(chunks):
        c_ao(q).wait()
        low = low + lax.dot_general(gath[q, z], aout_v[q], (((1,), (1,)), ((), ())), preferred_element_type=F32)
    lgg[z] = (low * mix[z]).astype(BF16)

    def lg_send(i):
        return remote(lgg.at[z], lgg.at[z], lg_s.at[i], lg_r.at[i], tensor=zpeer(i))

    def lg_recv(i):
        return remote(lgg.at[zfrom(i)], lgg.at[zfrom(i)], lg_s.at[i], lg_r.at[i], tensor=zpeer(i))

    each(nt - 1, lambda i: lg_send(i).start())

    def low_add(i):
        low_copy(i).wait_recv()
        lowp[z] += lowr[i]

    each(nt - 1, low_add)
    actg[z] = (lowp[z] * mix[z]).astype(BF16)

    def act_send(i):
        return remote(actg.at[z], actg.at[z], act_s.at[i], act_r.at[i], tensor=zpeer(i))

    def act_recv(i):
        return remote(actg.at[zfrom(i)], actg.at[zfrom(i)], act_s.at[i], act_r.at[i], tensor=zpeer(i))

    each(nt - 1, lambda i: act_send(i).start())
    if chunks > 1:
        gather_start(1)

    each(nt - 1, lambda i: lg_recv(i).wait_recv())
    low_grads = lgg[...].astype(F32).reshape(tokens, r).astype(BF16)
    part_a = lax.dot_general(hid_v[...], low_grads, (((0,), (0,)), ((), ())), preferred_element_type=F32)
    if nd * a_rows != ff:
        part_a = jnp.concatenate([part_a, jnp.zeros((nd * a_rows - ff, r), F32)], axis=0)
    part_a = part_a.reshape(nd, a_rows, r)
    paf[...] = part_a
    pab[...] = part_a.astype(BF16)

    def ra_copy(i):
        return remote(pab.at[dpeer(i)], par.at[i], ra_s.at[i], ra_r.at[i], dp=dpeer(i))

    each(nd - 1, lambda i: ra_copy(i).start())

    each(nt - 1, lambda i: act_recv(i).wait_recv())
    arrive(0)

    def gathered(q):
        return gath[q].astype(F32).reshape(tokens, dc).astype(BF16)

    acts = actg[...].astype(F32).reshape(tokens, r).astype(BF16)
    grads = gathered(0)
    part_b = lax.dot_general(acts, grads, (((0,), (0,)), ((), ())), preferred_element_type=F32)
    for i in range(nd):
        top, left = (i % piece_rows) * ROWS, (i // piece_rows) * dcp
        piece = part_b[top:top + ROWS, left:left + dcp]
        pbf[i] = piece
        pbb[i] = piece.astype(BF16)

    def rb_copy(i):
        return remote(pbb.at[dpeer(i)], pbr.at[i], rb_s.at[i], rb_r.at[i], dp=dpeer(i))

    each(nd - 1, lambda i: rb_copy(i).start())

    def product(q, grads):
        c_bd(q).wait()
        return lax.dot_general(grads, bd_v[q], (((1,), (1,)), ((), ())), preferred_element_type=F32)

    acc[...] = product(0, grads) + lax.dot_general(
        low_grads, ain_v[...], (((1,), (1,)), ((), ())), preferred_element_type=F32)

    def a_piece(owner):
        return a_out.at[pl.ds(pl.multiple_of(owner * a_rows, ROWS), a_rows), :]

    def aa_send(i):
        return remote(a_piece(d), a_piece(d), aa_s.at[i], aa_r.at[i], dp=dpeer(i))

    def aa_recv(i):
        return remote(a_piece(dfrom(i)), a_piece(dfrom(i)), aa_s.at[i], aa_r.at[i], dp=dpeer(i))

    def a_add(i):
        ra_copy(i).wait_recv()
        paf[d] += par[i].astype(F32)

    each(nd - 1, a_add)
    a_piece(d)[...] = paf[d].astype(BF16)
    each(nd - 1, lambda i: aa_send(i).start())

    def b_piece(owner_chip, owner_core, chunk):
        owner = owner_chip * 2 + owner_core
        top = pl.multiple_of(lax.rem(owner, piece_rows) * ROWS, ROWS)
        left = pl.multiple_of(chunk * dc + (owner // piece_rows) * dcp, LANES)
        return b_out.at[pl.ds(top, ROWS), pl.ds(left, dcp)]

    def chip_at(j):
        return lax.rem(chip + j, nc)

    def chunk_at(k):
        return lax.rem(zc + chunks - k, chunks)

    def b_add(i):
        rb_copy(i).wait_recv()
        pbf[d] += pbr[i].astype(F32)

    each(nd - 1, b_add)
    own_b = b_piece(chip, core, zc)
    own_b[...] = pbf[d].astype(BF16)

    def bz(k, part):
        return remote(part, part, bz_s.at[k], bz_r.at[k], tensor=zbase + lax.rem(zc + k + 1, chunks))

    def bx(j, k, part):
        return remote(part, part, bx_s.at[j, k], bx_r.at[j, k], dp=chip_at(j + 1) * 2 + core)

    def bc(j, k, part):
        return remote(part, part, bc_s.at[j, k], bc_r.at[j, k], dp=chip * 2 + 1 - core)

    each(chunks - 1, lambda k: bz(k, own_b).start())
    each(nc - 1, lambda j: bx(j, 0, own_b).start())
    bc(0, 0, own_b).start()

    for q in range(2, chunks):
        gather_start(q)

    def pass_on(k):
        def one(j):
            part = b_piece(lax.rem(chip + nc - j - 1, nc), core, chunk_at(k))
            bx(j, k, part).wait_recv()
            bc(j + 1, k, part).start()

        each(nc - 1, one)

    if chunks > 1:
        arrive(1)
        acc[...] += product(1, gathered(1))
    pass_on(0)
    for k in range(1, chunks):
        part = b_piece(chip, core, chunk_at(k))
        bz(k - 1, part).wait_recv()
        each(nc - 1, lambda j: bx(j, k, part).start())
        bc(0, k, part).start()
    if chunks > 2:
        arrive(2)
        acc[...] += product(2, gathered(2))
    for k in range(1, chunks):
        pass_on(k)
    for q in range(3, chunks):
        arrive(q)
        acc[...] += product(q, gathered(q))
    gh_out[...] = acc[...].astype(BF16)

    each(nd - 1, lambda i: aa_recv(i).wait_recv())
    for k in range(chunks):
        each(nc, lambda j: bc(j, k, b_piece(lax.rem(chip + nc - j, nc), 1 - core, chunk_at(k))).wait_recv())

    def z_sends(i):
        low_copy(i).wait_send()
        lg_send(i).wait_send()
        act_send(i).wait_send()
        for q in range(chunks):
            if_direct(q, i, functools.partial(lambda q: gather_send(q, i).wait_send(), q))

    each(nt - 1, z_sends)
    for q in range(chunks):
        passing(q, lambda c: c.wait_send())

    def d_sends(i):
        ra_copy(i).wait_send()
        rb_copy(i).wait_send()
        aa_send(i).wait_send()

    each(nd - 1, d_sends)
    each(chunks - 1, lambda k: bz(k, own_b).wait_send())
    for k in range(chunks):
        each(nc - 1, lambda j: bx(j, k, b_piece(chip, core, chunk_at(k))).wait_send())
        each(nc, lambda j: bc(j, k, b_piece(lax.rem(chip + nc - j, nc), core, chunk_at(k))).wait_send())


def finish(scale, gh, a, b, gh_out, a_out, b_out, a_v, b_v, sem):
    copies = [pltpu.make_async_copy(gh, gh_out, sem.at[0])]
    copies[0].start()
    step = b.shape[0] // 4
    for n in range(4):
        rows = pl.ds(n * step, step)
        b_v[rows, :] = b[rows, :].astype(F32) * scale
        copies.append(pltpu.make_async_copy(b_v.at[rows, :], b_out.at[rows, :], sem.at[1 + n]))
        copies[-1].start()
    a_v[...] = a[:a_v.shape[0], :].astype(F32) * scale
    copies.append(pltpu.make_async_copy(a_v, a_out, sem.at[5]))
    copies[-1].start()
    for c in copies:
        c.wait()


def shards(nd, nt, hidden, grad_out, base_down, adapter_in, adapter_out, mix_ids, comp_index, comp_coef):
    tokens, ff = hidden.shape
    tg, width = grad_out.shape
    r = adapter_in.shape[1]
    piece_rows, piece_cols, chunks = plan(nd, nt, width, r)
    dc = width // chunks
    dcp = dc // piece_cols
    a_rows = -(-ff // (nd * ROWS)) * ROWS
    grad_scale = float(tokens * nd) ** (-0.5)
    hbm = pl.BlockSpec(memory_space=pltpu.HBM)
    vmem = pl.BlockSpec(memory_space=pltpu.VMEM)
    dma = pltpu.SemaphoreType.DMA
    zs, ds = max(nt - 1, 1), max(nd - 1, 1)
    scratch = [
        pltpu.VMEM((tokens, ff), BF16), pltpu.VMEM((ff, r), BF16),
        pltpu.VMEM((1, tokens), jnp.int32), pltpu.VMEM((PICKS, COMBOS), jnp.int32), pltpu.VMEM((PICKS, COMBOS), F32),
        pltpu.VMEM((chunks, r, dc), BF16),
        pltpu.VMEM((chunks, ff, dc), BF16), pltpu.VMEM((chunks, nt, tg, dc), BF16),
        pltpu.VMEM((nt, tg, r), F32), pltpu.VMEM((nt, tg, r), F32), pltpu.VMEM((zs, tg, r), F32),
        pltpu.VMEM((nt, tg, r), BF16), pltpu.VMEM((nt, tg, r), BF16),
        pltpu.VMEM((nd, a_rows, r), F32), pltpu.VMEM((nd, a_rows, r), BF16), pltpu.VMEM((ds, a_rows, r), BF16),
        pltpu.VMEM((nd, ROWS, dcp), F32), pltpu.VMEM((nd, ROWS, dcp), BF16), pltpu.VMEM((ds, ROWS, dcp), BF16),
        pltpu.VMEM((tokens, ff), F32),
        dma((5,)), dma((chunks,)), dma((chunks,)), dma((chunks,)),
        dma((zs,)), dma((zs,)), dma((chunks, zs)), dma((chunks, zs)), dma((chunks, 2)), dma((zs,)), dma((zs,)), dma((zs,)), dma((zs,)),
        dma((ds,)), dma((ds,)), dma((ds,)), dma((ds,)), dma((ds,)), dma((ds,)),
        dma((chunks,)), dma((chunks,)), dma((nd // 2, chunks)), dma((nd // 2, chunks)),
        dma((nd // 2, chunks)), dma((nd // 2, chunks)),
    ]
    grad_hidden, sum_a, sum_b = pl.pallas_call(
        functools.partial(kernel, nd, nt),
        out_shape=(
            jax.ShapeDtypeStruct((tokens, ff), BF16),
            jax.ShapeDtypeStruct((nd * a_rows, r), BF16),
            jax.ShapeDtypeStruct((r, width), BF16),
        ),
        in_specs=[hbm] * 8,
        out_specs=(vmem, vmem, vmem),
        scratch_shapes=scratch,
        compiler_params=pltpu.CompilerParams(
            collective_id=0, has_side_effects=True, vmem_limit_bytes=48 * 1024 * 1024),
    )(hidden, grad_out, base_down, adapter_in, adapter_out, mix_ids.reshape(1, tokens), comp_index.T, comp_coef.T)
    return pl.pallas_call(
        functools.partial(finish, grad_scale),
        out_shape=(
            jax.ShapeDtypeStruct((tokens, ff), BF16),
            jax.ShapeDtypeStruct((ff, r), F32),
            jax.ShapeDtypeStruct((r, width), F32),
        ),
        in_specs=[vmem] * 3,
        out_specs=(hbm, hbm, hbm),
        scratch_shapes=[pltpu.VMEM((ff, r), F32), pltpu.VMEM((r, width), F32), dma((6,))],
        compiler_params=pltpu.CompilerParams(vmem_limit_bytes=16 * 1024 * 1024),
    )(grad_hidden, sum_a, sum_b)


def solution(mesh):
    in_specs = (
        P("dp", "tensor"),
        P(("dp", "tensor"), None),
        P("tensor", None),
        P("tensor", None),
        P(),
        P("dp"),
        P(),
        P(),
    )
    out_specs = (P("dp", "tensor"), P("tensor", None), P())
    body = functools.partial(shards, mesh.shape["dp"], mesh.shape["tensor"])
    return jax.shard_map(body, mesh=mesh, in_specs=in_specs, out_specs=out_specs, check_vma=False)
```

```python
import functools

import jax
import jax.numpy as jnp
from jax import lax
from jax.experimental import pallas as pl
from jax.experimental.pallas import tpu as pltpu
from jax.sharding import PartitionSpec as P

RANK = 16
COMBOS = 16
PICKS = 2
LANES = 128
ROWS = 16
F32 = jnp.float32
BF16 = jnp.bfloat16
MESH = pl.DeviceIdType.MESH


def each(count, body):
    if count <= 8:
        for i in range(count):
            body(i)
    else:
        pl.loop(0, count)(body)


def plan(nd, nt, width, r):
    piece_rows = min(nd, r // ROWS)
    piece_cols = nd // piece_rows
    chunks = max(c for c in range(1, nt + 1) if nt % c == 0 and width % (LANES * c * piece_cols) == 0)
    return piece_rows, piece_cols, chunks


def kernel(nd, nt, hid, go, bd, ain, aout, ids, cidx, ccoef,
           gh_out, a_out, b_out,
           hid_v, ain_v, ids_v, cidx_v, ccoef_v, aout_v, bd_v, gath, mix, lowp, lowr, lgg, actg, paf, pab, par, pbf, pbb, pbr, acc,
           loc, loc_go, loc_ao, loc_bd, low_s, low_r, gat_s, gat_r, fwd_s, lg_s, lg_r, act_s, act_r,
           ra_s, ra_r, rb_s, rb_r, aa_s, aa_r, bz_s, bz_r, bx_s, bx_r, bc_s, bc_r):
    d, z = lax.axis_index("dp"), lax.axis_index("tensor")
    tg, width = go.shape
    tokens, ff = hid.shape
    r = ain.shape[1]
    piece_rows, piece_cols, chunks = plan(nd, nt, width, r)
    dc = width // chunks
    dcp = dc // piece_cols
    zc = lax.rem(z, chunks)
    zbase = z - zc
    nc = nd // 2
    chip, core = d // 2, lax.rem(d, 2)
    a_rows = pab.shape[1]

    half = (nt + 1) // 2
    turn = 1 - 2 * (z // half)

    def columns(k):
        return pl.ds(pl.multiple_of(lax.rem(zc + turn * k + chunks, chunks) * dc, LANES), dc)

    def zpeer(i):
        return lax.rem(z + i + 1, nt)

    def zfrom(i):
        return lax.rem(z + nt - i - 1, nt)

    def dpeer(i):
        return lax.rem(d + i + 1, nd)

    def dfrom(i):
        return lax.rem(d + nd - i - 1, nd)

    def remote(src, dst, send, recv, **where):
        return pltpu.make_async_remote_copy(
            src_ref=src, dst_ref=dst, send_sem=send, recv_sem=recv, device_id=where, device_id_type=MESH)

    c_hid = pltpu.make_async_copy(hid, hid_v, loc.at[0])
    c_ain = pltpu.make_async_copy(ain, ain_v, loc.at[1])

    def c_go(q):
        return pltpu.make_async_copy(go.at[:, columns(q)], gath.at[q, z], loc_go.at[q])

    def c_ao(q):
        return pltpu.make_async_copy(aout.at[:, columns(q)], aout_v.at[q], loc_ao.at[q])

    def c_bd(q):
        return pltpu.make_async_copy(bd.at[:, columns(q)], bd_v.at[q], loc_bd.at[q])

    small = [pltpu.make_async_copy(src, dst, loc.at[2 + n])
             for n, (src, dst) in enumerate(((ids, ids_v), (cidx, cidx_v), (ccoef, ccoef_v)))]
    c_hid.start()
    c_ain.start()
    for c in small:
        c.start()
    each(chunks, lambda q: c_go(q).start())
    each(chunks, lambda q: c_ao(q).start())
    each(chunks, lambda q: c_bd(q).start())

    barrier = pltpu.get_barrier_semaphore()
    each(nt - 1, lambda i: pl.semaphore_signal(barrier, inc=1, device_id={"tensor": zpeer(i)}, device_id_type=MESH))
    each(nd - 1, lambda i: pl.semaphore_signal(barrier, inc=1, device_id={"dp": dpeer(i)}, device_id_type=MESH))

    row = lax.broadcasted_iota(jnp.int32, (r, COMBOS), 0)
    table = jnp.zeros((r, COMBOS), F32)
    for c in small:
        c.wait()
    for p in range(PICKS):
        first = cidx_v[p:p + 1, :] * RANK
        table = table + jnp.where((row >= first) & (row < first + RANK), ccoef_v[p:p + 1, :], 0.0)
    one_hot = (lax.broadcasted_iota(jnp.int32, (COMBOS, tokens), 0) == ids_v[...]).astype(F32)
    mix_t = jnp.dot(table, one_hot, precision=lax.Precision.HIGHEST, preferred_element_type=F32)
    mix[...] = mix_t.T.reshape(nt, tg, r)

    c_hid.wait()
    c_ain.wait()
    lowp[...] = jnp.dot(hid_v[...], ain_v[...], preferred_element_type=F32).reshape(nt, tg, r)
    each(chunks, lambda q: c_go(q).wait())

    pl.semaphore_wait(barrier, nt + nd - 2)

    def low_copy(i):
        return remote(lowp.at[zpeer(i)], lowr.at[i], low_s.at[i], low_r.at[i], tensor=zpeer(i))

    each(nt - 1, lambda i: low_copy(i).start())

    def gather_send(q, i):
        there = zpeer(i)
        chunk = lax.rem(lax.rem(there, chunks) + (1 - 2 * (there // half)) * q + chunks, chunks)
        mine = lax.rem(turn * (chunk - zc) + chunks, chunks)
        return remote(gath.at[mine, z], gath.at[q, z], gat_s.at[q, i], gat_r.at[q, i], tensor=zpeer(i))

    def gather_recv(q, i):
        return remote(gath.at[q, zfrom(i)], gath.at[q, zfrom(i)], gat_s.at[q, i], gat_r.at[q, i], tensor=zpeer(i))

    def if_direct(q, i, act):
        if q == 0 or nt < 3:
            act()
        else:
            pl.when(jnp.logical_not(((z == 0) & (i == nt - 2)) | ((z == nt - 1) & (i == 0))))(act)

    def gather_start(q):
        each(nt - 1, lambda i: if_direct(q, i, lambda: gather_send(q, i).start()))

    def passing(q, act):
        if nt >= 3 and q + 1 < chunks:
            for side, (via, src, end, i) in enumerate(((nt - 2, 0, nt - 1, nt - 2), (1, nt - 1, 0, 0))):
                pl.when(z == via)(functools.partial(act, remote(
                    gath.at[q, src], gath.at[q + 1, src], fwd_s.at[q, side], gat_r.at[q + 1, i], tensor=end)))

    def arrive(q):
        each(nt - 1, lambda i: gather_recv(q, i).wait_recv())
        passing(q, lambda c: c.start())

    gather_start(0)

    low = jnp.zeros((tg, r), F32)
    for q in range(chunks):
        c_ao(q).wait()
        low = low + lax.dot_general(gath[q, z], aout_v[q], (((1,), (1,)), ((), ())), preferred_element_type=F32)
    lgg[z] = (low * mix[z]).astype(BF16)

    def lg_send(i):
        return remote(lgg.at[z], lgg.at[z], lg_s.at[i], lg_r.at[i], tensor=zpeer(i))

    def lg_recv(i):
        return remote(lgg.at[zfrom(i)], lgg.at[zfrom(i)], lg_s.at[i], lg_r.at[i], tensor=zpeer(i))

    each(nt - 1, lambda i: lg_send(i).start())

    def low_add(i):
        low_copy(i).wait_recv()
        lowp[z] += lowr[i]

    each(nt - 1, low_add)
    actg[z] = (lowp[z] * mix[z]).astype(BF16)

    def act_send(i):
        return remote(actg.at[z], actg.at[z], act_s.at[i], act_r.at[i], tensor=zpeer(i))

    def act_recv(i):
        return remote(actg.at[zfrom(i)], actg.at[zfrom(i)], act_s.at[i], act_r.at[i], tensor=zpeer(i))

    each(nt - 1, lambda i: act_send(i).start())
    if chunks > 1:
        gather_start(1)

    each(nt - 1, lambda i: act_recv(i).wait_recv())
    arrive(0)

    def gathered(q):
        return gath[q].astype(F32).reshape(tokens, dc).astype(BF16)

    acts = actg[...].astype(F32).reshape(tokens, r).astype(BF16)
    grads = gathered(0)
    part_b = lax.dot_general(acts, grads, (((0,), (0,)), ((), ())), preferred_element_type=F32)
    for i in range(nd):
        top, left = (i % piece_rows) * ROWS, (i // piece_rows) * dcp
        piece = part_b[top:top + ROWS, left:left + dcp]
        pbf[i] = piece
        pbb[i] = piece.astype(BF16)

    def rb_copy(i):
        return remote(pbb.at[dpeer(i)], pbr.at[i], rb_s.at[i], rb_r.at[i], dp=dpeer(i))

    each(nd - 1, lambda i: rb_copy(i).start())

    each(nt - 1, lambda i: lg_recv(i).wait_recv())
    low_grads = lgg[...].astype(F32).reshape(tokens, r).astype(BF16)
    part_a = lax.dot_general(hid_v[...], low_grads, (((0,), (0,)), ((), ())), preferred_element_type=F32)
    if nd * a_rows != ff:
        part_a = jnp.concatenate([part_a, jnp.zeros((nd * a_rows - ff, r), F32)], axis=0)
    part_a = part_a.reshape(nd, a_rows, r)
    paf[...] = part_a
    pab[...] = part_a.astype(BF16)

    def ra_copy(i):
        return remote(pab.at[dpeer(i)], par.at[i], ra_s.at[i], ra_r.at[i], dp=dpeer(i))

    each(nd - 1, lambda i: ra_copy(i).start())

    def product(q, grads):
        c_bd(q).wait()
        return lax.dot_general(grads, bd_v[q], (((1,), (1,)), ((), ())), preferred_element_type=F32)

    acc[...] = product(0, grads) + lax.dot_general(
        low_grads, ain_v[...], (((1,), (1,)), ((), ())), preferred_element_type=F32)

    def a_piece(owner):
        return a_out.at[pl.ds(pl.multiple_of(owner * a_rows, ROWS), a_rows), :]

    def aa_send(i):
        return remote(a_piece(d), a_piece(d), aa_s.at[i], aa_r.at[i], dp=dpeer(i))

    def aa_recv(i):
        return remote(a_piece(dfrom(i)), a_piece(dfrom(i)), aa_s.at[i], aa_r.at[i], dp=dpeer(i))

    def b_piece(owner_chip, owner_core, chunk):
        owner = owner_chip * 2 + owner_core
        top = pl.multiple_of(lax.rem(owner, piece_rows) * ROWS, ROWS)
        left = pl.multiple_of(chunk * dc + (owner // piece_rows) * dcp, LANES)
        return b_out.at[pl.ds(top, ROWS), pl.ds(left, dcp)]

    def chip_at(j):
        return lax.rem(chip + j, nc)

    def chunk_at(k):
        return lax.rem(zc + chunks - k, chunks)

    def b_add(i):
        rb_copy(i).wait_recv()
        pbf[d] += pbr[i].astype(F32)

    each(nd - 1, b_add)
    own_b = b_piece(chip, core, zc)
    own_b[...] = pbf[d].astype(BF16)

    def bz(k, part):
        return remote(part, part, bz_s.at[k], bz_r.at[k], tensor=zbase + lax.rem(zc + k + 1, chunks))

    def bx(j, k, part):
        return remote(part, part, bx_s.at[j, k], bx_r.at[j, k], dp=chip_at(j + 1) * 2 + core)

    def bc(j, k, part):
        return remote(part, part, bc_s.at[j, k], bc_r.at[j, k], dp=chip * 2 + 1 - core)

    each(chunks - 1, lambda k: bz(k, own_b).start())
    each(nc - 1, lambda j: bx(j, 0, own_b).start())
    bc(0, 0, own_b).start()

    for q in range(2, chunks):
        gather_start(q)

    def a_add(i):
        ra_copy(i).wait_recv()
        paf[d] += par[i].astype(F32)

    each(nd - 1, a_add)
    a_piece(d)[...] = paf[d].astype(BF16)
    each(nd - 1, lambda i: aa_send(i).start())

    def pass_on(k):
        def one(j):
            part = b_piece(lax.rem(chip + nc - j - 1, nc), core, chunk_at(k))
            bx(j, k, part).wait_recv()
            bc(j + 1, k, part).start()

        each(nc - 1, one)

    if chunks > 1:
        arrive(1)
        acc[...] += product(1, gathered(1))
    pass_on(0)
    for k in range(1, chunks):
        part = b_piece(chip, core, chunk_at(k))
        bz(k - 1, part).wait_recv()
        each(nc - 1, lambda j: bx(j, k, part).start())
        bc(0, k, part).start()
    if chunks > 2:
        arrive(2)
        acc[...] += product(2, gathered(2))
    for k in range(1, chunks):
        pass_on(k)
    for q in range(3, chunks):
        arrive(q)
        acc[...] += product(q, gathered(q))
    gh_out[...] = acc[...].astype(BF16)

    each(nd - 1, lambda i: aa_recv(i).wait_recv())
    for k in range(chunks):
        each(nc, lambda j: bc(j, k, b_piece(lax.rem(chip + nc - j, nc), 1 - core, chunk_at(k))).wait_recv())

    def z_sends(i):
        low_copy(i).wait_send()
        lg_send(i).wait_send()
        act_send(i).wait_send()
        for q in range(chunks):
            if_direct(q, i, functools.partial(lambda q: gather_send(q, i).wait_send(), q))

    each(nt - 1, z_sends)
    for q in range(chunks):
        passing(q, lambda c: c.wait_send())

    def d_sends(i):
        ra_copy(i).wait_send()
        rb_copy(i).wait_send()
        aa_send(i).wait_send()

    each(nd - 1, d_sends)
    each(chunks - 1, lambda k: bz(k, own_b).wait_send())
    for k in range(chunks):
        each(nc - 1, lambda j: bx(j, k, b_piece(chip, core, chunk_at(k))).wait_send())
        each(nc, lambda j: bc(j, k, b_piece(lax.rem(chip + nc - j, nc), core, chunk_at(k))).wait_send())


def finish(scale, gh, a, b, gh_out, a_out, b_out, a_v, b_v, sem):
    copies = [pltpu.make_async_copy(gh, gh_out, sem.at[0])]
    copies[0].start()
    step = b.shape[0] // 4
    for n in range(4):
        rows = pl.ds(n * step, step)
        b_v[rows, :] = b[rows, :].astype(F32) * scale
        copies.append(pltpu.make_async_copy(b_v.at[rows, :], b_out.at[rows, :], sem.at[1 + n]))
        copies[-1].start()
    a_v[...] = a[:a_v.shape[0], :].astype(F32) * scale
    copies.append(pltpu.make_async_copy(a_v, a_out, sem.at[5]))
    copies[-1].start()
    for c in copies:
        c.wait()


def shards(nd, nt, hidden, grad_out, base_down, adapter_in, adapter_out, mix_ids, comp_index, comp_coef):
    tokens, ff = hidden.shape
    tg, width = grad_out.shape
    r = adapter_in.shape[1]
    piece_rows, piece_cols, chunks = plan(nd, nt, width, r)
    dc = width // chunks
    dcp = dc // piece_cols
    a_rows = -(-ff // (nd * ROWS)) * ROWS
    grad_scale = float(tokens * nd) ** (-0.5)
    hbm = pl.BlockSpec(memory_space=pltpu.HBM)
    vmem = pl.BlockSpec(memory_space=pltpu.VMEM)
    dma = pltpu.SemaphoreType.DMA
    zs, ds = max(nt - 1, 1), max(nd - 1, 1)
    scratch = [
        pltpu.VMEM((tokens, ff), BF16), pltpu.VMEM((ff, r), BF16),
        pltpu.VMEM((1, tokens), jnp.int32), pltpu.VMEM((PICKS, COMBOS), jnp.int32), pltpu.VMEM((PICKS, COMBOS), F32),
        pltpu.VMEM((chunks, r, dc), BF16),
        pltpu.VMEM((chunks, ff, dc), BF16), pltpu.VMEM((chunks, nt, tg, dc), BF16),
        pltpu.VMEM((nt, tg, r), F32), pltpu.VMEM((nt, tg, r), F32), pltpu.VMEM((zs, tg, r), F32),
        pltpu.VMEM((nt, tg, r), BF16), pltpu.VMEM((nt, tg, r), BF16),
        pltpu.VMEM((nd, a_rows, r), F32), pltpu.VMEM((nd, a_rows, r), BF16), pltpu.VMEM((ds, a_rows, r), BF16),
        pltpu.VMEM((nd, ROWS, dcp), F32), pltpu.VMEM((nd, ROWS, dcp), BF16), pltpu.VMEM((ds, ROWS, dcp), BF16),
        pltpu.VMEM((tokens, ff), F32),
        dma((5,)), dma((chunks,)), dma((chunks,)), dma((chunks,)),
        dma((zs,)), dma((zs,)), dma((chunks, zs)), dma((chunks, zs)), dma((chunks, 2)), dma((zs,)), dma((zs,)), dma((zs,)), dma((zs,)),
        dma((ds,)), dma((ds,)), dma((ds,)), dma((ds,)), dma((ds,)), dma((ds,)),
        dma((chunks,)), dma((chunks,)), dma((nd // 2, chunks)), dma((nd // 2, chunks)),
        dma((nd // 2, chunks)), dma((nd // 2, chunks)),
    ]
    grad_hidden, sum_a, sum_b = pl.pallas_call(
        functools.partial(kernel, nd, nt),
        out_shape=(
            pltpu.VMEM((tokens, ff), BF16),
            pltpu.VMEM((nd * a_rows, r), BF16),
            pltpu.VMEM((r, width), BF16),
        ),
        in_specs=[hbm] * 8,
        out_specs=(vmem, vmem, vmem),
        scratch_shapes=scratch,
        compiler_params=pltpu.CompilerParams(
            collective_id=0, has_side_effects=True, vmem_limit_bytes=56 * 1024 * 1024),
    )(hidden, grad_out, base_down, adapter_in, adapter_out, mix_ids.reshape(1, tokens), comp_index.T, comp_coef.T)
    return pl.pallas_call(
        functools.partial(finish, grad_scale),
        out_shape=(
            jax.ShapeDtypeStruct((tokens, ff), BF16),
            jax.ShapeDtypeStruct((ff, r), F32),
            jax.ShapeDtypeStruct((r, width), F32),
        ),
        in_specs=[vmem] * 3,
        out_specs=(hbm, hbm, hbm),
        scratch_shapes=[pltpu.VMEM((ff, r), F32), pltpu.VMEM((r, width), F32), dma((6,))],
        compiler_params=pltpu.CompilerParams(vmem_limit_bytes=16 * 1024 * 1024),
    )(grad_hidden, sum_a, sum_b)


def solution(mesh):
    in_specs = (
        P("dp", "tensor"),
        P(("dp", "tensor"), None),
        P("tensor", None),
        P("tensor", None),
        P(),
        P("dp"),
        P(),
        P(),
    )
    out_specs = (P("dp", "tensor"), P("tensor", None), P())
    body = functools.partial(shards, mesh.shape["dp"], mesh.shape["tensor"])
    return jax.shard_map(body, mesh=mesh, in_specs=in_specs, out_specs=out_specs, check_vma=False)
```

```python
import functools

import jax
import jax.numpy as jnp
from jax import lax
from jax.experimental import pallas as pl
from jax.experimental.pallas import tpu as pltpu
from jax.sharding import PartitionSpec as P

RANK = 16
COMBOS = 16
PICKS = 2
LANES = 128
ROWS = 16
F32 = jnp.float32
BF16 = jnp.bfloat16
MESH = pl.DeviceIdType.MESH


def each(count, body):
    if count <= 8:
        for i in range(count):
            body(i)
    else:
        pl.loop(0, count)(body)


def plan(nd, nt, width, r):
    piece_rows = min(nd, r // ROWS)
    piece_cols = nd // piece_rows
    chunks = max(c for c in range(1, nt + 1) if nt % c == 0 and width % (LANES * c * piece_cols) == 0)
    return piece_rows, piece_cols, chunks


def kernel(nd, nt, hid, go, bd, ain, aout, ids, cidx, ccoef,
           gh_out, a_out, b_out,
           hid_v, ain_v, ids_v, cidx_v, ccoef_v, aout_v, bd_v, gath, mix, lowp, lowr, lgg, actg, paf, pab, par, pbf, pbb, pbr, acc,
           loc, loc_go, loc_ao, loc_bd, low_s, low_r, gat_s, gat_r, fwd_s, lg_s, lg_r, act_s, act_r,
           ra_s, ra_r, rb_s, rb_r, aa_s, aa_r, bz_s, bz_r, bx_s, bx_r, bc_s, bc_r):
    d, z = lax.axis_index("dp"), lax.axis_index("tensor")
    tg, width = go.shape
    tokens, ff = hid.shape
    r = ain.shape[1]
    piece_rows, piece_cols, chunks = plan(nd, nt, width, r)
    dc = width // chunks
    dcp = dc // piece_cols
    zc = lax.rem(z, chunks)
    zbase = z - zc
    nc = nd // 2
    chip, core = d // 2, lax.rem(d, 2)
    a_rows = pab.shape[1]

    half = (nt + 1) // 2
    turn = 1 - 2 * (z // half)

    def columns(k):
        return pl.ds(pl.multiple_of(lax.rem(zc + turn * k + chunks, chunks) * dc, LANES), dc)

    def zpeer(i):
        return lax.rem(z + i + 1, nt)

    def zfrom(i):
        return lax.rem(z + nt - i - 1, nt)

    def dpeer(i):
        return lax.rem(d + i + 1, nd)

    def dfrom(i):
        return lax.rem(d + nd - i - 1, nd)

    def remote(src, dst, send, recv, **where):
        return pltpu.make_async_remote_copy(
            src_ref=src, dst_ref=dst, send_sem=send, recv_sem=recv, device_id=where, device_id_type=MESH)

    c_hid = pltpu.make_async_copy(hid, hid_v, loc.at[0])
    c_ain = pltpu.make_async_copy(ain, ain_v, loc.at[1])

    def c_go(q):
        return pltpu.make_async_copy(go.at[:, columns(q)], gath.at[q, z], loc_go.at[q])

    def c_ao(q):
        return pltpu.make_async_copy(aout.at[:, columns(q)], aout_v.at[q], loc_ao.at[q])

    def c_bd(q):
        return pltpu.make_async_copy(bd.at[:, columns(q)], bd_v.at[q], loc_bd.at[q])

    small = [pltpu.make_async_copy(src, dst, loc.at[2 + n])
             for n, (src, dst) in enumerate(((ids, ids_v), (cidx, cidx_v), (ccoef, ccoef_v)))]
    c_hid.start()
    c_ain.start()
    for c in small:
        c.start()
    each(chunks, lambda q: c_go(q).start())
    each(chunks, lambda q: c_ao(q).start())
    each(chunks, lambda q: c_bd(q).start())

    barrier = pltpu.get_barrier_semaphore()
    each(nt - 1, lambda i: pl.semaphore_signal(barrier, inc=1, device_id={"tensor": zpeer(i)}, device_id_type=MESH))
    each(nd - 1, lambda i: pl.semaphore_signal(barrier, inc=1, device_id={"dp": dpeer(i)}, device_id_type=MESH))

    row = lax.broadcasted_iota(jnp.int32, (r, COMBOS), 0)
    table = jnp.zeros((r, COMBOS), F32)
    for c in small:
        c.wait()
    for p in range(PICKS):
        first = cidx_v[p:p + 1, :] * RANK
        table = table + jnp.where((row >= first) & (row < first + RANK), ccoef_v[p:p + 1, :], 0.0)
    one_hot = (lax.broadcasted_iota(jnp.int32, (COMBOS, tokens), 0) == ids_v[...]).astype(F32)
    mix_t = jnp.dot(table, one_hot, precision=lax.Precision.HIGHEST, preferred_element_type=F32)
    mix[...] = mix_t.T.reshape(nt, tg, r)

    c_hid.wait()
    c_ain.wait()
    lowp[...] = jnp.dot(hid_v[...], ain_v[...], preferred_element_type=F32).reshape(nt, tg, r)
    each(chunks, lambda q: c_go(q).wait())

    pl.semaphore_wait(barrier, nt + nd - 2)

    def low_copy(i):
        return remote(lowp.at[zpeer(i)], lowr.at[i], low_s.at[i], low_r.at[i], tensor=zpeer(i))

    each(nt - 1, lambda i: low_copy(i).start())

    def gather_send(q, i):
        there = zpeer(i)
        chunk = lax.rem(lax.rem(there, chunks) + (1 - 2 * (there // half)) * q + chunks, chunks)
        mine = lax.rem(turn * (chunk - zc) + chunks, chunks)
        return remote(gath.at[mine, z], gath.at[q, z], gat_s.at[q, i], gat_r.at[q, i], tensor=zpeer(i))

    def gather_recv(q, i):
        return remote(gath.at[q, zfrom(i)], gath.at[q, zfrom(i)], gat_s.at[q, i], gat_r.at[q, i], tensor=zpeer(i))

    def if_direct(q, i, act):
        if q == 0 or nt < 3:
            act()
        else:
            pl.when(jnp.logical_not(((z == 0) & (i == nt - 2)) | ((z == nt - 1) & (i == 0))))(act)

    def gather_start(q):
        each(nt - 1, lambda i: if_direct(q, i, lambda: gather_send(q, i).start()))

    def passing(q, act):
        if nt >= 3 and q + 1 < chunks:
            for side, (via, src, end, i) in enumerate(((nt - 2, 0, nt - 1, nt - 2), (1, nt - 1, 0, 0))):
                pl.when(z == via)(functools.partial(act, remote(
                    gath.at[q, src], gath.at[q + 1, src], fwd_s.at[q, side], gat_r.at[q + 1, i], tensor=end)))

    def arrive(q):
        each(nt - 1, lambda i: gather_recv(q, i).wait_recv())
        passing(q, lambda c: c.start())

    gather_start(0)

    low = jnp.zeros((tg, r), F32)
    for q in range(chunks):
        c_ao(q).wait()
        low = low + lax.dot_general(gath[q, z], aout_v[q], (((1,), (1,)), ((), ())), preferred_element_type=F32)
    lgg[z] = (low * mix[z]).astype(BF16)

    def lg_send(i):
        return remote(lgg.at[z], lgg.at[z], lg_s.at[i], lg_r.at[i], tensor=zpeer(i))

    def lg_recv(i):
        return remote(lgg.at[zfrom(i)], lgg.at[zfrom(i)], lg_s.at[i], lg_r.at[i], tensor=zpeer(i))

    each(nt - 1, lambda i: lg_send(i).start())

    def low_add(i):
        low_copy(i).wait_recv()
        lowp[z] += lowr[i]

    each(nt - 1, low_add)
    actg[z] = (lowp[z] * mix[z]).astype(BF16)

    def act_send(i):
        return remote(actg.at[z], actg.at[z], act_s.at[i], act_r.at[i], tensor=zpeer(i))

    def act_recv(i):
        return remote(actg.at[zfrom(i)], actg.at[zfrom(i)], act_s.at[i], act_r.at[i], tensor=zpeer(i))

    each(nt - 1, lambda i: act_send(i).start())
    if chunks > 1:
        gather_start(1)
    for q in range(2, chunks):
        gather_start(q)

    each(nt - 1, lambda i: lg_recv(i).wait_recv())
    low_grads = lgg[...].astype(F32).reshape(tokens, r).astype(BF16)
    part_a = lax.dot_general(hid_v[...], low_grads, (((0,), (0,)), ((), ())), preferred_element_type=F32)
    if nd * a_rows != ff:
        part_a = jnp.concatenate([part_a, jnp.zeros((nd * a_rows - ff, r), F32)], axis=0)
    part_a = part_a.reshape(nd, a_rows, r)
    paf[...] = part_a
    pab[...] = part_a.astype(BF16)

    each(nt - 1, lambda i: act_recv(i).wait_recv())
    arrive(0)

    def gathered(q):
        return gath[q].astype(F32).reshape(tokens, dc).astype(BF16)

    acts = actg[...].astype(F32).reshape(tokens, r).astype(BF16)
    grads = gathered(0)
    part_b = lax.dot_general(acts, grads, (((0,), (0,)), ((), ())), preferred_element_type=F32)
    for i in range(nd):
        top, left = (i % piece_rows) * ROWS, (i // piece_rows) * dcp
        piece = part_b[top:top + ROWS, left:left + dcp]
        pbf[i] = piece
        pbb[i] = piece.astype(BF16)

    def rb_copy(i):
        return remote(pbb.at[dpeer(i)], pbr.at[i], rb_s.at[i], rb_r.at[i], dp=dpeer(i))

    each(nd - 1, lambda i: rb_copy(i).start())

    def ra_copy(i):
        return remote(pab.at[dpeer(i)], par.at[i], ra_s.at[i], ra_r.at[i], dp=dpeer(i))

    each(nd - 1, lambda i: ra_copy(i).start())

    def product(q, grads):
        c_bd(q).wait()
        return lax.dot_general(grads, bd_v[q], (((1,), (1,)), ((), ())), preferred_element_type=F32)

    acc[...] = product(0, grads) + lax.dot_general(
        low_grads, ain_v[...], (((1,), (1,)), ((), ())), preferred_element_type=F32)

    def a_piece(owner):
        return a_out.at[pl.ds(pl.multiple_of(owner * a_rows, ROWS), a_rows), :]

    def aa_send(i):
        return remote(a_piece(d), a_piece(d), aa_s.at[i], aa_r.at[i], dp=dpeer(i))

    def aa_recv(i):
        return remote(a_piece(dfrom(i)), a_piece(dfrom(i)), aa_s.at[i], aa_r.at[i], dp=dpeer(i))

    def b_piece(owner_chip, owner_core, chunk):
        owner = owner_chip * 2 + owner_core
        top = pl.multiple_of(lax.rem(owner, piece_rows) * ROWS, ROWS)
        left = pl.multiple_of(chunk * dc + (owner // piece_rows) * dcp, LANES)
        return b_out.at[pl.ds(top, ROWS), pl.ds(left, dcp)]

    def chip_at(j):
        return lax.rem(chip + j, nc)

    def chunk_at(k):
        return lax.rem(zc + chunks - k, chunks)

    def b_add(i):
        rb_copy(i).wait_recv()
        pbf[d] += pbr[i].astype(F32)

    each(nd - 1, b_add)
    own_b = b_piece(chip, core, zc)
    own_b[...] = pbf[d].astype(BF16)

    def bz(k, part):
        return remote(part, part, bz_s.at[k], bz_r.at[k], tensor=zbase + lax.rem(zc + k + 1, chunks))

    def bx(j, k, part):
        return remote(part, part, bx_s.at[j, k], bx_r.at[j, k], dp=chip_at(j + 1) * 2 + core)

    def bc(j, k, part):
        return remote(part, part, bc_s.at[j, k], bc_r.at[j, k], dp=chip * 2 + 1 - core)

    each(chunks - 1, lambda k: bz(k, own_b).start())
    each(nc - 1, lambda j: bx(j, 0, own_b).start())
    bc(0, 0, own_b).start()


    def a_add(i):
        ra_copy(i).wait_recv()
        paf[d] += par[i].astype(F32)

    each(nd - 1, a_add)
    a_piece(d)[...] = paf[d].astype(BF16)
    each(nd - 1, lambda i: aa_send(i).start())

    def pass_on(k):
        def one(j):
            part = b_piece(lax.rem(chip + nc - j - 1, nc), core, chunk_at(k))
            bx(j, k, part).wait_recv()
            bc(j + 1, k, part).start()

        each(nc - 1, one)

    if chunks > 1:
        arrive(1)
        acc[...] += product(1, gathered(1))
    pass_on(0)
    for k in range(1, chunks):
        part = b_piece(chip, core, chunk_at(k))
        bz(k - 1, part).wait_recv()
        each(nc - 1, lambda j: bx(j, k, part).start())
        bc(0, k, part).start()
    if chunks > 2:
        arrive(2)
        acc[...] += product(2, gathered(2))
    for k in range(1, chunks):
        pass_on(k)
    for q in range(3, chunks):
        arrive(q)
        acc[...] += product(q, gathered(q))
    gh_out[...] = acc[...].astype(BF16)

    each(nd - 1, lambda i: aa_recv(i).wait_recv())
    for k in range(chunks):
        each(nc, lambda j: bc(j, k, b_piece(lax.rem(chip + nc - j, nc), 1 - core, chunk_at(k))).wait_recv())

    def z_sends(i):
        low_copy(i).wait_send()
        lg_send(i).wait_send()
        act_send(i).wait_send()
        for q in range(chunks):
            if_direct(q, i, functools.partial(lambda q: gather_send(q, i).wait_send(), q))

    each(nt - 1, z_sends)
    for q in range(chunks):
        passing(q, lambda c: c.wait_send())

    def d_sends(i):
        ra_copy(i).wait_send()
        rb_copy(i).wait_send()
        aa_send(i).wait_send()

    each(nd - 1, d_sends)
    each(chunks - 1, lambda k: bz(k, own_b).wait_send())
    for k in range(chunks):
        each(nc - 1, lambda j: bx(j, k, b_piece(chip, core, chunk_at(k))).wait_send())
        each(nc, lambda j: bc(j, k, b_piece(lax.rem(chip + nc - j, nc), core, chunk_at(k))).wait_send())


def finish(scale, gh, a, b, gh_out, a_out, b_out, a_v, b_v, sem):
    copies = [pltpu.make_async_copy(gh, gh_out, sem.at[0])]
    copies[0].start()
    step = b.shape[0] // 4
    for n in range(4):
        rows = pl.ds(n * step, step)
        b_v[rows, :] = b[rows, :].astype(F32) * scale
        copies.append(pltpu.make_async_copy(b_v.at[rows, :], b_out.at[rows, :], sem.at[1 + n]))
        copies[-1].start()
    a_v[...] = a[:a_v.shape[0], :].astype(F32) * scale
    copies.append(pltpu.make_async_copy(a_v, a_out, sem.at[5]))
    copies[-1].start()
    for c in copies:
        c.wait()


def shards(nd, nt, hidden, grad_out, base_down, adapter_in, adapter_out, mix_ids, comp_index, comp_coef):
    tokens, ff = hidden.shape
    tg, width = grad_out.shape
    r = adapter_in.shape[1]
    piece_rows, piece_cols, chunks = plan(nd, nt, width, r)
    dc = width // chunks
    dcp = dc // piece_cols
    a_rows = -(-ff // (nd * ROWS)) * ROWS
    grad_scale = float(tokens * nd) ** (-0.5)
    hbm = pl.BlockSpec(memory_space=pltpu.HBM)
    vmem = pl.BlockSpec(memory_space=pltpu.VMEM)
    dma = pltpu.SemaphoreType.DMA
    zs, ds = max(nt - 1, 1), max(nd - 1, 1)
    scratch = [
        pltpu.VMEM((tokens, ff), BF16), pltpu.VMEM((ff, r), BF16),
        pltpu.VMEM((1, tokens), jnp.int32), pltpu.VMEM((PICKS, COMBOS), jnp.int32), pltpu.VMEM((PICKS, COMBOS), F32),
        pltpu.VMEM((chunks, r, dc), BF16),
        pltpu.VMEM((chunks, ff, dc), BF16), pltpu.VMEM((chunks, nt, tg, dc), BF16),
        pltpu.VMEM((nt, tg, r), F32), pltpu.VMEM((nt, tg, r), F32), pltpu.VMEM((zs, tg, r), F32),
        pltpu.VMEM((nt, tg, r), BF16), pltpu.VMEM((nt, tg, r), BF16),
        pltpu.VMEM((nd, a_rows, r), F32), pltpu.VMEM((nd, a_rows, r), BF16), pltpu.VMEM((ds, a_rows, r), BF16),
        pltpu.VMEM((nd, ROWS, dcp), F32), pltpu.VMEM((nd, ROWS, dcp), BF16), pltpu.VMEM((ds, ROWS, dcp), BF16),
        pltpu.VMEM((tokens, ff), F32),
        dma((5,)), dma((chunks,)), dma((chunks,)), dma((chunks,)),
        dma((zs,)), dma((zs,)), dma((chunks, zs)), dma((chunks, zs)), dma((chunks, 2)), dma((zs,)), dma((zs,)), dma((zs,)), dma((zs,)),
        dma((ds,)), dma((ds,)), dma((ds,)), dma((ds,)), dma((ds,)), dma((ds,)),
        dma((chunks,)), dma((chunks,)), dma((nd // 2, chunks)), dma((nd // 2, chunks)),
        dma((nd // 2, chunks)), dma((nd // 2, chunks)),
    ]
    grad_hidden, sum_a, sum_b = pl.pallas_call(
        functools.partial(kernel, nd, nt),
        out_shape=(
            pltpu.VMEM((tokens, ff), BF16),
            pltpu.VMEM((nd * a_rows, r), BF16),
            pltpu.VMEM((r, width), BF16),
        ),
        in_specs=[hbm] * 8,
        out_specs=(vmem, vmem, vmem),
        scratch_shapes=scratch,
        compiler_params=pltpu.CompilerParams(
            collective_id=0, has_side_effects=True, vmem_limit_bytes=56 * 1024 * 1024),
    )(hidden, grad_out, base_down, adapter_in, adapter_out, mix_ids.reshape(1, tokens), comp_index.T, comp_coef.T)
    return pl.pallas_call(
        functools.partial(finish, grad_scale),
        out_shape=(
            jax.ShapeDtypeStruct((tokens, ff), BF16),
            jax.ShapeDtypeStruct((ff, r), F32),
            jax.ShapeDtypeStruct((r, width), F32),
        ),
        in_specs=[vmem] * 3,
        out_specs=(hbm, hbm, hbm),
        scratch_shapes=[pltpu.VMEM((ff, r), F32), pltpu.VMEM((r, width), F32), dma((6,))],
        compiler_params=pltpu.CompilerParams(vmem_limit_bytes=16 * 1024 * 1024),
    )(grad_hidden, sum_a, sum_b)


def solution(mesh):
    in_specs = (
        P("dp", "tensor"),
        P(("dp", "tensor"), None),
        P("tensor", None),
        P("tensor", None),
        P(),
        P("dp"),
        P(),
        P(),
    )
    out_specs = (P("dp", "tensor"), P("tensor", None), P())
    body = functools.partial(shards, mesh.shape["dp"], mesh.shape["tensor"])
    return jax.shard_map(body, mesh=mesh, in_specs=in_specs, out_specs=out_specs, check_vma=False)
```
